1024 devices in a mesh: box: 4 (over x_hi, core), dir: 256 (over y, x_lo, z).
Axes of the slice: x: 4 (x_hi: 2, x_lo: 2; x = x_hi * 2 + x_lo), y: 4, z: 32, core: 2. Of those that a mesh axis runs over, the one named last changes fastest.
Arguments:
- patterns: float32 [4, 2048, 64, 256], P('box', 'dir'), may hold values from -4 to 4
- far_boxes: int32 [256, 32, 16], P('dir'), may hold values from 0 to 31
- far_types: int32 [256, 32, 16], P('dir'), may hold values from 0 to 315
- transfer: bfloat16 [316, 64, 256], P(None, 'box'), may hold values from -1.5 to 1.5
Outputs:
- incoming: float32 [256, 32, 64, 256], P('dir', None, 'box')
- aggregated: float32 [1024, 128, 512], P('dir', 'box')
The draws below stay inside these ranges and needn't reach their ends.
All inputs are finite; a program needn't handle non-finite values.
Results may differ from the reference program's by a relative error of at most 0.0003.
Values sent between devices are 32-bit elements; how exact they have to be, the bound alone decides.
A program may use at most 64 MiB of HBM per device.

```python
import math
import jax
import jax.numpy as jnp
from jax import lax

TH = 64
PHI = 128
BOX_DEV = 8
LEVELS = 3
FAR = 16
NTYPES = 316
GROUP = 32
SLAB_BOXES = 2048
PARENTS = 4
N_BOX = 4
N_DIR = 256


def with_ends(values, stream_key, least, top_value):
    extent = values.shape
    index_at = [jax.random.randint(jax.random.fold_in(stream_key, axis), (), 0, extent[axis]) for axis in range(len(extent))]
    values = values.at[tuple(index_at)].set(least)
    longest = extent.index(max(extent))
    index_at[longest] = (index_at[longest] + 1) % extent[longest]
    return values.at[tuple(index_at)].set(top_value)


def levels(rng, dims, pieces, low, high):
    level = 1.0
    for position, parts in pieces:
        steps = jax.random.uniform(jax.random.fold_in(jax.random.fold_in(rng, 6), position), (parts,), jnp.float32, low / len(pieces), high / len(pieces))
        level = level * jnp.repeat(jnp.exp(steps), dims[position] // parts).reshape((-1,) + (1,) * (len(dims) - 1 - position))
    return level


def normal_values(key, dims, width, limit, split=(), kind=jnp.bfloat16):
    entries = jax.random.normal(key, dims, jnp.float32) * width
    if len(split) > 0:
        entries = levels(key, dims, split, -0.22, 0.18) * entries
    return jnp.clip(entries, min=-limit, max=limit).astype(kind)


def setup_inputs(seed: int = 0) -> dict:
    seeds = jax.random.split(jax.random.key(seed), 5)
    return {
        "patterns": normal_values(seeds[0], (N_BOX, SLAB_BOXES, TH, 2 * PHI), 0.5, 4.0, ((0, 4), (1, 256)), jnp.float32),
        "far_boxes": with_ends(jax.random.randint(seeds[1], (N_DIR, GROUP, FAR), 0, GROUP), jax.random.fold_in(seeds[1], 1), 0, GROUP - 1).astype(jnp.int32),
        "far_types": with_ends(jax.random.randint(seeds[2], (N_DIR, GROUP, FAR), 0, NTYPES), jax.random.fold_in(seeds[2], 1), 0, NTYPES - 1).astype(jnp.int32),
        "transfer": normal_values(seeds[3], (NTYPES, TH, 2 * PHI), 0.25, 1.5, ((1, 4),)),
    }


two_pi = 2.0 * math.pi
step_phase = 8.0
outer_weight = -0.0390625
inner_weight = 0.2734375
center_weight = 0.8203125
across_weight = -0.0546875


def interp_table(azimuth):
    orders = jnp.arange(azimuth // 2 + 1, dtype=jnp.int32)
    source_index = jnp.arange(azimuth, dtype=jnp.int32)
    target_index = jnp.arange(2 * azimuth, dtype=jnp.int32)
    source_angle = (two_pi / azimuth) * ((orders[:, None] * source_index[None, :]) % azimuth).astype(jnp.float32)
    target_angle = (two_pi / (2 * azimuth)) * ((orders[:, None] * target_index[None, :]) % (2 * azimuth)).astype(jnp.float32)
    weights = jnp.where((orders == 0) | (orders == azimuth // 2), 1.0, 2.0).astype(jnp.float32) / azimuth
    cosine_part = jnp.dot((jnp.cos(source_angle) * weights[:, None]).T, jnp.cos(target_angle), precision=lax.Precision.HIGHEST, preferred_element_type=jnp.float32)
    sine_part = jnp.dot((jnp.sin(source_angle) * weights[:, None]).T, jnp.sin(target_angle), precision=lax.Precision.HIGHEST, preferred_element_type=jnp.float32)
    return cosine_part + sine_part


def phase_angle(level_num, first_row, row_count, polar_count, azimuth):
    polar_angle = (math.pi / polar_count) * ((first_row + jnp.arange(row_count, dtype=jnp.int32)).astype(jnp.float32) + 0.5)
    azimuth_angle = (two_pi / azimuth) * jnp.arange(azimuth, dtype=jnp.int32).astype(jnp.float32)
    pick_axis = (level_num - 1) % 3
    if pick_axis == 0:
        direction = jnp.sin(polar_angle)[:, None] * jnp.cos(azimuth_angle)[None, :]
    elif pick_axis == 1:
        direction = jnp.sin(polar_angle)[:, None] * jnp.sin(azimuth_angle)[None, :]
    else:
        direction = jnp.cos(polar_angle)[:, None] * jnp.ones((1, azimuth), jnp.float32)
    return step_phase * direction


def rotate(widened, rotation):
    cosine = jnp.cos(rotation)
    sine_part = jnp.sin(rotation)
    real_part = widened[..., 0, :]
    imag_part = widened[..., 1, :]
    return jnp.concatenate([cosine * real_part - sine_part * imag_part, sine_part * real_part + cosine * imag_part], axis=-1)


def shift_terms(block, rotation):
    half_span = block.shape[-1] // 2
    split_parts = block.reshape(block.shape[:-1] + (2, half_span))
    return rotate(split_parts, rotation)


def complex_product(left_side, right_side):
    half_span = left_side.shape[-1] // 2
    left_real = left_side[..., :half_span]
    left_imag = left_side[..., half_span:]
    right_real = right_side[..., :half_span]
    right_imag = right_side[..., half_span:]
    return jnp.concatenate([left_real * right_real - left_imag * right_imag, left_real * right_imag + left_imag * right_real], axis=-1)


def reflect_rows(block):
    half_span = block.shape[-1] // 2
    split_parts = block.reshape(block.shape[:-1] + (2, half_span))
    return jnp.roll(split_parts, half_span // 2, axis=-1).reshape(block.shape)


def pole_extend(slab):
    row_count = slab.shape[-2]
    top_rows = reflect_rows(slab[..., 0:2, :][..., ::-1, :])
    bottom_rows = reflect_rows(slab[..., row_count - 2:, :][..., ::-1, :])
    return jnp.concatenate([top_rows, slab, bottom_rows], axis=-2)


def polar_refine(extended):
    row_count = extended.shape[-2] - 4

    def rows_at(offset):
        return extended[..., offset:offset + row_count, :]

    even_rows = outer_weight * rows_at(0) + inner_weight * rows_at(1) + center_weight * rows_at(2) + across_weight * rows_at(3)
    odd_rows = across_weight * rows_at(1) + center_weight * rows_at(2) + inner_weight * rows_at(3) + outer_weight * rows_at(4)
    paired = jnp.stack([even_rows, odd_rows], axis=-2)
    return paired.reshape(extended.shape[:-2] + (2 * row_count, extended.shape[-1]))


def azimuth_refine(block, interp_matrix):
    half_span = block.shape[-1] // 2
    split_parts = block.reshape(block.shape[:-1] + (2, half_span))
    widened = jnp.einsum("...cw,wv->...cv", split_parts, interp_matrix, precision=lax.Precision.HIGHEST, preferred_element_type=jnp.float32)
    return widened.reshape(block.shape[:-1] + (4 * half_span,))


def pick_rows(slab_rows, row_index):
    return slab_rows[row_index]


def translate(slab_data, far_boxes, far_types, operator_rows):
    def add_term(term_index, running):
        chosen = jax.vmap(pick_rows)(slab_data, far_boxes[:, :, term_index])
        operator_part = operator_rows[far_types[:, :, term_index]].astype(jnp.float32)
        return running + complex_product(operator_part, chosen)

    start_value = jnp.zeros(slab_data.shape, jnp.float32)
    return lax.fori_loop(0, FAR, add_term, start_value)


def merge_level(block, level_num, angle_full):
    slab_count, slot_count, row_count, sample_span = block.shape
    lower = 2 ** (level_num - 1)
    side_bit = ((jnp.arange(slab_count, dtype=jnp.int32) // lower) % 2).astype(jnp.float32)
    flip_sign = 2.0 * side_bit - 1.0
    terms = shift_terms(block, flip_sign[:, None, None, None] * angle_full[None, None, :, :])
    shaped = terms.reshape(slab_count // (2 * lower), 2, lower, N_BOX, 2, slot_count // (2 * N_BOX), row_count, sample_span)
    summed = shaped[:, 0] + shaped[:, 1]
    return summed.transpose(0, 3, 1, 2, 4, 5, 6).reshape(slab_count, slot_count // 2, row_count, sample_span)


def reference(patterns, far_boxes, far_types, transfer):
    regrouped = patterns.reshape(N_BOX, N_DIR, BOX_DEV, TH, 2 * PHI).transpose(1, 0, 2, 3, 4).reshape(N_DIR, GROUP, TH, 2 * PHI)
    interp_matrix = interp_table(PHI)
    angles = [phase_angle(level_index + 1, 0, 2 * TH, 2 * TH, 2 * PHI) for level_index in range(LEVELS)]

    def per_row(polar_row):
        slab_data = lax.dynamic_index_in_dim(regrouped, polar_row, 2, keepdims=False)
        operator_rows = lax.dynamic_index_in_dim(transfer, polar_row, 1, keepdims=False)
        return translate(slab_data, far_boxes, far_types, operator_rows)

    incoming_rows = lax.map(per_row, jnp.arange(TH, dtype=jnp.int32))
    incoming = incoming_rows.transpose(1, 2, 0, 3)

    def per_block(block_index):
        block = lax.dynamic_slice_in_dim(regrouped, (block_index * 8).astype(jnp.int32), 8, 0)
        merged = azimuth_refine(polar_refine(pole_extend(block)), interp_matrix)
        for level_index in range(LEVELS):
            merged = merge_level(merged, level_index + 1, angles[level_index])
        return merged

    merged_blocks = lax.map(per_block, jnp.arange(N_DIR // 8, dtype=jnp.int32))
    aggregated = merged_blocks.reshape(N_DIR * PARENTS, 2 * TH, 4 * PHI)
    return (incoming, aggregated)
```

```python
import math

import jax
import jax.numpy as jnp
from jax import lax
from jax.experimental import pallas as pl
from jax.experimental.pallas import tpu as pltpu
from jax.sharding import PartitionSpec as P

MESH = pl.DeviceIdType.MESH
F32, BF16 = jnp.float32, jnp.bfloat16

TH, PHI, BOXES, FAR, GROUP, OCTET, N_BOX = 64, 128, 8, 16, 32, 8, 4
SLAB = TH // N_BOX
CHUNKS = 4
ROWS = (24, 16, 16, 8)
ASCENDING = (0, 24, 40, 56)
DESCENDING = (40, 24, 8, 0)

two_pi = 2.0 * math.pi
step_phase = 8.0
outer_weight = -0.0390625
inner_weight = 0.2734375
center_weight = 0.8203125
across_weight = -0.0546875


def halves(value):
    high = value.astype(BF16)
    return high, (value - high.astype(F32)).astype(BF16)


def index_like(shape, dim):
    return lax.broadcasted_iota(jnp.int32, shape, dim)


def interp_tables(high_ref, low_ref):
    shape = (PHI, 2 * PHI)
    apart = 2 * index_like(shape, 0) - index_like(shape, 1)
    odd = lax.rem(apart + 2 * PHI, 2) == 1
    sign = jnp.where(lax.rem(apart + 2 * PHI, 4) == 1, 1.0, -1.0)
    angle = (math.pi / (2 * PHI)) * apart.astype(F32)
    value = sign * jnp.cos(angle) / (PHI * jnp.where(odd, jnp.sin(angle), 1.0))
    value = jnp.where(odd, value, jnp.where(apart == 0, 1.0, 0.0))
    high, low = halves(value)
    high_ref[0:PHI] = high
    high_ref[PHI : 2 * PHI] = high
    low_ref[...] = low


def phase_tables(signs, lateral, axial):
    shape = (2 * TH, 2 * PHI)
    polar = (math.pi / (2 * TH)) * (index_like(shape, 0).astype(F32) + 0.5)
    azimuth = (two_pi / (2 * PHI)) * index_like(shape, 1).astype(F32)
    sine = step_phase * jnp.sin(polar)
    first, second = sine * jnp.cos(azimuth), sine * jnp.sin(azimuth)
    cos_1, sin_1 = jnp.cos(first), signs[0] * jnp.sin(first)
    cos_2, sin_2 = jnp.cos(second), signs[1] * jnp.sin(second)
    lateral[0] = cos_1 * cos_2
    lateral[1] = sin_1 * cos_2
    lateral[2] = cos_1 * sin_2
    lateral[3] = sin_1 * sin_2
    third = step_phase * jnp.cos(polar)
    axial[0] = jnp.cos(third)
    axial[1] = signs[2] * jnp.sin(third)


def polar_weights(slab):
    shape = (2 * SLAB, 4 * SLAB)
    row, column = index_like(shape, 0), lax.rem(index_like(shape, 1), 2 * SLAB)
    column = jnp.where((slab == 0) & (column < 8), 7 - column, column)
    column = jnp.where((slab == N_BOX - 1) & (column >= 24), 55 - column, column)
    offset = column - 8 - row // 2
    flipped = jnp.where(lax.rem(row, 2) == 0, offset, -offset)
    weights = jnp.zeros(shape, F32)
    for place, weight in ((-2, outer_weight), (-1, inner_weight), (0, center_weight), (1, across_weight)):
        weights = jnp.where(flipped == place, weight, weights)
    return weights.astype(BF16)


def kernel(
    pat, far_boxes, far_types, transfer, incoming, aggregated,
    ext, slab, ops, inc, made, kept, fb, ft, high, low, lateral, axial,
    z_send, z_recv, x_send, x_recv, a_send, a_recv, local,
):
    q, r = lax.axis_index("box"), lax.axis_index("dir")
    l = lax.rem(r, OCTET)
    base = r - l
    bits = (lax.rem(l, 2), lax.rem(l // 2, 2), l // 4)
    upper, core = q // 2, lax.rem(q, 2)

    def sibling(d):
        n = [b if not d >> s & 1 else 1 - b for s, b in enumerate(bits)]
        return base + n[0] + 2 * n[1] + 4 * n[2], 4 * n[0] + 2 * n[1] + n[2]

    def box_peer(e):
        c = 1 - core if e & 1 else core
        u = 1 - upper if e & 2 else upper
        return 2 * u + c

    barrier = pltpu.get_barrier_semaphore()
    for d in range(1, OCTET):
        pl.semaphore_signal(barrier, inc=1, device_id=(q, sibling(d)[0]), device_id_type=MESH)
    for e in range(1, N_BOX):
        pl.semaphore_signal(barrier, inc=1, device_id=(box_peer(e), r), device_id_type=MESH)

    locals_ = [
        pltpu.make_async_copy(far_boxes.at[0], fb, local.at[0]),
        pltpu.make_async_copy(far_types.at[0], ft, local.at[1]),
        pltpu.make_async_copy(transfer, ops, local.at[2]),
        pltpu.make_async_copy(pat.at[0, sibling(0)[1]], ext.at[0, pl.ds(8, TH)], local.at[3]),
        pltpu.make_async_copy(
            pat.at[0, :, pl.ds(pl.multiple_of(SLAB * q, 8), SLAB)],
            slab.at[pl.ds(BOXES * q, BOXES)],
            local.at[4],
        ),
    ]
    for copy in locals_:
        copy.start()
    pl.semaphore_wait(barrier, OCTET - 1 + N_BOX - 1)

    def z_copy(c, d):
        other, box = sibling(d)
        first = pl.multiple_of(upper * ASCENDING[c] + (1 - upper) * DESCENDING[c], 8)
        return pltpu.make_async_remote_copy(
            src_ref=pat.at[0, box, pl.ds(first, ROWS[c])],
            dst_ref=ext.at[d, pl.ds(pl.multiple_of(8 + first, 8), ROWS[c])],
            send_sem=z_send.at[c, d],
            recv_sem=z_recv.at[c, d],
            device_id=(q, other),
            device_id_type=MESH,
        )

    def x_copy(e):
        other = box_peer(e)
        return pltpu.make_async_remote_copy(
            src_ref=pat.at[0, :, pl.ds(pl.multiple_of(SLAB * other, 8), SLAB)],
            dst_ref=slab.at[pl.ds(BOXES * q, BOXES)],
            send_sem=x_send.at[e],
            recv_sem=x_recv.at[e],
            device_id=(other, r),
            device_id_type=MESH,
        )

    def a_copy(c):
        target = upper * c + (1 - upper) * (N_BOX - 1 - c)
        return pltpu.make_async_remote_copy(
            src_ref=made.at[c],
            dst_ref=kept.at[q],
            send_sem=a_send.at[c],
            recv_sem=a_recv.at[q],
            device_id=(target, r),
            device_id_type=MESH,
        )

    order = (7, 6, 5, 4, 3, 2, 1)
    z_copies = [[z_copy(c, d) for d in order] for c in range(CHUNKS)]
    x_copies = [x_copy(e) for e in (3, 2, 1)]
    for copy in z_copies[0] + x_copies + z_copies[1] + z_copies[2] + z_copies[3]:
        copy.start()

    signs = [2.0 * b.astype(F32) - 1.0 for b in bits]
    interp_tables(high, low)
    phase_tables(signs, lateral, axial)

    def translation():
        for copy in (locals_[0], locals_[1], locals_[2], locals_[4]):
            copy.wait()
        for copy in x_copies:
            copy.wait_recv()

        def one_box(g, carry):
            real = jnp.zeros((SLAB, PHI), F32)
            imag = jnp.zeros((SLAB, PHI), F32)
            for k in range(FAR):
                box, kind = fb[g, k], ft[g, k]
                value = slab[box]
                factor = ops[kind].astype(F32)
                value_r, value_i = value[:, :PHI], value[:, PHI:]
                factor_r, factor_i = factor[:, :PHI], factor[:, PHI:]
                real += factor_r * value_r - factor_i * value_i
                imag += factor_r * value_i + factor_i * value_r
            inc[g, :, 0:PHI] = real
            inc[g, :, PHI : 2 * PHI] = imag
            return carry

        lax.fori_loop(0, GROUP, one_box, 0)
        out = pltpu.make_async_copy(inc, incoming.at[0], local.at[5])
        out.start()
        return out

    def refine(c):
        target = upper * c + (1 - upper) * (N_BOX - 1 - c)
        if c in (0, CHUNKS - 1):
            bottom = 1 - upper if c == 0 else upper
            source = pl.multiple_of(8 + bottom * (TH - 8), 8)
            place = pl.multiple_of(bottom * (TH + 8), 8)
            for d in range(OCTET):
                rows = ext[d, pl.ds(source, 8), :]
                ext[d, pl.ds(place, 8), 0:PHI] = pltpu.roll(rows[:, :PHI], PHI // 2, 1)
                ext[d, pl.ds(place, 8), PHI : 2 * PHI] = pltpu.roll(rows[:, PHI:], PHI // 2, 1)
        window = pl.ds(pl.multiple_of(SLAB * target, 8), 2 * SLAB)
        sums = [ext[d, window, :] for d in range(OCTET)]
        for s in (1, 2, 4):
            sums = [sums[k] + sums[k ^ s] if not k & s else sums[k ^ s] - sums[k] for k in range(OCTET)]
        weights = polar_weights(target)
        rows = []
        for k in range(OCTET):
            pieces = jnp.concatenate(halves(sums[k]), axis=0)
            polar = jnp.dot(weights, pieces, preferred_element_type=F32)
            rows += [polar[:, :PHI], polar[:, PHI:]]
        stacked_high, stacked_low = halves(jnp.concatenate(rows, axis=0))
        both = jnp.concatenate([stacked_high, stacked_low], axis=1)
        wide = jnp.dot(both, high[...], preferred_element_type=F32)
        wide += jnp.dot(stacked_high, low[...], preferred_element_type=F32)
        angles = pl.ds(pl.multiple_of(2 * SLAB * target, 8), 2 * SLAB)
        parts = []
        for third in range(2):
            real, imag = 0.0, 0.0
            for k in range(4):
                at = 4 * SLAB * (4 * third + k)
                w_r = wide[at : at + 2 * SLAB]
                w_i = wide[at + 2 * SLAB : at + 4 * SLAB]
                table = lateral[k, angles, :]
                if k == 0:
                    real, imag = table * w_r, table * w_i
                elif k == 3:
                    real, imag = real - table * w_r, imag - table * w_i
                else:
                    real, imag = real - table * w_i, imag + table * w_r
            parts.append((real, imag))
        cosine, sine = axial[0, angles, :], axial[1, angles, :]
        made[c, :, 0 : 2 * PHI] = cosine * parts[0][0] - sine * parts[1][1]
        made[c, :, 2 * PHI : 4 * PHI] = cosine * parts[0][1] + sine * parts[1][0]

        @pl.when(target != q)
        def _():
            a_copy(c).start()

        @pl.when(target == q)
        def _():
            kept[q] = made[c]

    locals_[3].wait()
    inc_out = None
    for c in range(CHUNKS):
        for copy in z_copies[c]:
            copy.wait_recv()
        refine(c)
        if c == 1:
            inc_out = translation()

    for e in range(1, N_BOX):
        other = box_peer(e)
        pltpu.make_async_remote_copy(
            src_ref=made.at[0],
            dst_ref=kept.at[other],
            send_sem=a_send.at[0],
            recv_sem=a_recv.at[other],
            device_id=(other, r),
            device_id_type=MESH,
        ).wait_recv()
    agg_out = pltpu.make_async_copy(kept, aggregated, local.at[6])
    agg_out.start()
    for c in range(CHUNKS):
        target = upper * c + (1 - upper) * (N_BOX - 1 - c)

        @pl.when(target != q)
        def _():
            a_copy(c).wait_send()

        for copy in z_copies[c]:
            copy.wait_send()
    for copy in x_copies:
        copy.wait_send()
    inc_out.wait()
    agg_out.wait()


def shards(patterns, far_boxes, far_types, transfer):
    anywhere = pl.BlockSpec(memory_space=pl.ANY)
    vmem = pltpu.VMEM
    dma = pltpu.SemaphoreType.DMA
    return pl.pallas_call(
        kernel,
        out_shape=(
            jax.ShapeDtypeStruct((1, GROUP, SLAB, 2 * PHI), F32),
            jax.ShapeDtypeStruct((N_BOX, 2 * SLAB, 4 * PHI), F32),
        ),
        in_specs=[anywhere] * 4,
        out_specs=(anywhere, anywhere),
        scratch_shapes=[
            vmem((OCTET, TH + 16, 2 * PHI), F32),
            vmem((GROUP, SLAB, 2 * PHI), F32),
            vmem(transfer.shape, BF16),
            vmem((GROUP, SLAB, 2 * PHI), F32),
            vmem((CHUNKS, 2 * SLAB, 4 * PHI), F32),
            vmem((N_BOX, 2 * SLAB, 4 * PHI), F32),
            pltpu.SMEM((GROUP, FAR), jnp.int32),
            pltpu.SMEM((GROUP, FAR), jnp.int32),
            vmem((2 * PHI, 2 * PHI), BF16),
            vmem((PHI, 2 * PHI), BF16),
            vmem((4, 2 * TH, 2 * PHI), F32),
            vmem((2, 2 * TH, 2 * PHI), F32),
            dma((CHUNKS, OCTET)),
            dma((CHUNKS, OCTET)),
            dma((N_BOX,)),
            dma((N_BOX,)),
            dma((CHUNKS,)),
            dma((N_BOX,)),
            dma((7,)),
        ],
        compiler_params=pltpu.CompilerParams(
            collective_id=0, has_side_effects=True, vmem_limit_bytes=48 * 1024 * 1024
        ),
    )(patterns, far_boxes, far_types, transfer)


def solution(mesh):
    return jax.shard_map(
        shards,
        mesh=mesh,
        in_specs=(
            P("box", "dir", None, None),
            P("dir", None, None),
            P("dir", None, None),
            P(None, "box", None),
        ),
        out_specs=(P("dir", None, "box", None), P("dir", "box", None)),
        check_vma=False,
    )
```

```python
import math

import jax
import jax.numpy as jnp
from jax import lax
from jax.experimental import pallas as pl
from jax.experimental.pallas import tpu as pltpu
from jax.sharding import PartitionSpec as P

MESH = pl.DeviceIdType.MESH
F32, BF16 = jnp.float32, jnp.bfloat16

TH, PHI, BOXES, FAR, GROUP, OCTET, N_BOX = 64, 128, 8, 16, 32, 8, 4
SLAB = TH // N_BOX
CHUNKS = 4
ROWS = (24, 16, 16, 8)
ASCENDING = (0, 24, 40, 56)
DESCENDING = (40, 24, 8, 0)

two_pi = 2.0 * math.pi
step_phase = 8.0
outer_weight = -0.0390625
inner_weight = 0.2734375
center_weight = 0.8203125
across_weight = -0.0546875


def halves(value):
    high = value.astype(BF16)
    return high, (value - high.astype(F32)).astype(BF16)


def index_like(shape, dim):
    return lax.broadcasted_iota(jnp.int32, shape, dim)


def interp_tables(high_ref, low_ref):
    shape = (PHI, 2 * PHI)
    apart = 2 * index_like(shape, 0) - index_like(shape, 1)
    odd = lax.rem(apart + 2 * PHI, 2) == 1
    sign = jnp.where(lax.rem(apart + 2 * PHI, 4) == 1, 1.0, -1.0)
    angle = (math.pi / (2 * PHI)) * apart.astype(F32)
    value = sign * jnp.cos(angle) / (PHI * jnp.where(odd, jnp.sin(angle), 1.0))
    value = jnp.where(odd, value, jnp.where(apart == 0, 1.0, 0.0))
    high, low = halves(value)
    high_ref[0:PHI] = high
    high_ref[PHI : 2 * PHI] = high
    low_ref[...] = low


def phase_tables(lateral, axial):
    shape = (2 * TH, 2 * PHI)
    polar = (math.pi / (2 * TH)) * (index_like(shape, 0).astype(F32) + 0.5)
    azimuth = (two_pi / (2 * PHI)) * index_like(shape, 1).astype(F32)
    sine = step_phase * jnp.sin(polar)
    first, second = sine * jnp.cos(azimuth), sine * jnp.sin(azimuth)
    cos_1, sin_1 = jnp.cos(first), jnp.sin(first)
    cos_2, sin_2 = jnp.cos(second), jnp.sin(second)
    lateral[0] = cos_1 * cos_2
    lateral[1] = sin_1 * cos_2
    lateral[2] = cos_1 * sin_2
    lateral[3] = sin_1 * sin_2
    third = step_phase * jnp.cos(polar)
    axial[0] = jnp.cos(third)
    axial[1] = jnp.sin(third)


def polar_weights(slab):
    shape = (2 * SLAB, 4 * SLAB)
    row, column = index_like(shape, 0), lax.rem(index_like(shape, 1), 2 * SLAB)
    column = jnp.where((slab == 0) & (column < 8), 7 - column, column)
    column = jnp.where((slab == N_BOX - 1) & (column >= 24), 55 - column, column)
    offset = column - 8 - row // 2
    flipped = jnp.where(lax.rem(row, 2) == 0, offset, -offset)
    weights = jnp.zeros(shape, F32)
    for place, weight in ((-2, outer_weight), (-1, inner_weight), (0, center_weight), (1, across_weight)):
        weights = jnp.where(flipped == place, weight, weights)
    return weights.astype(BF16)


def kernel(
    pat, far_boxes, far_types, transfer, incoming, kept,
    ext, slab, ops, made, fb, ft, high, low, lateral, axial,
    known, known_box, z_send, z_recv, x_send, x_recv, a_send, a_recv, local,
):
    q, r = lax.axis_index("box"), lax.axis_index("dir")
    place = lax.rem(r, OCTET)
    base = r - place
    upper, core = q // 2, lax.rem(q, 2)

    def kept_box(p):
        return 4 * lax.rem(p, 2) + 2 * lax.rem(p // 2, 2) + p // 4

    def box_peer(e):
        c = 1 - core if e & 1 else core
        u = 1 - upper if e & 2 else upper
        return 2 * u + c

    def tell(semaphore, p):
        pl.semaphore_signal(semaphore, inc=1, device_id=(q, base + p), device_id_type=MESH)

    barrier = pltpu.get_barrier_semaphore()

    staggered = lax.rem(r // OCTET, 4) < 2
    together = jnp.logical_not(staggered)
    rank = lax.rem(place + OCTET - 1, OCTET)
    ranked = [(p, (p + OCTET - 1) % OCTET) for p in (1, 2, 3, 4, 5, 6, 7, 0)]

    for p, other in ranked:

        @pl.when((other > rank) | (together & (other < rank)))
        def _():
            tell(barrier, p)

    def tell_box(semaphore, other):
        pl.semaphore_signal(semaphore, inc=1, device_id=(other, r), device_id_type=MESH)

    for b in range(N_BOX - 1):

        @pl.when(b < q)
        def _():
            tell_box(barrier, b)

    for b in range(1, N_BOX):

        @pl.when(together & (b > q))
        def _():
            tell_box(barrier, b)

    locals_ = [
        pltpu.make_async_copy(far_boxes.at[0], fb, local.at[0]),
        pltpu.make_async_copy(far_types.at[0], ft, local.at[1]),
        pltpu.make_async_copy(transfer, ops, local.at[2]),
        pltpu.make_async_copy(pat.at[0, kept_box(place)], ext.at[place, pl.ds(8, TH)], local.at[3]),
        pltpu.make_async_copy(
            pat.at[0, :, pl.ds(pl.multiple_of(SLAB * q, 8), SLAB)],
            slab.at[pl.ds(BOXES * q, BOXES)],
            local.at[4],
        ),
    ]
    for copy in locals_:
        copy.start()
    expected = jnp.where(together, OCTET - 1 + N_BOX - 1, rank + N_BOX - 1 - q)

    @pl.when(expected > 0)
    def _():
        pl.semaphore_wait(barrier, expected)

    for p, other in ranked:

        @pl.when(staggered & (other < rank))
        def _():
            tell(known.at[place], p)

    for b in range(1, N_BOX):

        @pl.when(staggered & (b > q))
        def _():
            tell_box(known_box.at[q], b)

    def z_copy(c, p):
        first = pl.multiple_of(upper * ASCENDING[c] + (1 - upper) * DESCENDING[c], 8)
        return pltpu.make_async_remote_copy(
            src_ref=pat.at[0, kept_box(p), pl.ds(first, ROWS[c])],
            dst_ref=ext.at[place, pl.ds(pl.multiple_of(8 + first, 8), ROWS[c])],
            send_sem=z_send.at[c, p],
            recv_sem=z_recv.at[c, place],
            device_id=(q, base + p),
            device_id_type=MESH,
        )

    def z_arrival(c, p):
        first = pl.multiple_of(upper * ASCENDING[c] + (1 - upper) * DESCENDING[c], 8)
        return pltpu.make_async_remote_copy(
            src_ref=pat.at[0, 0, pl.ds(first, ROWS[c])],
            dst_ref=ext.at[p, pl.ds(pl.multiple_of(8 + first, 8), ROWS[c])],
            send_sem=z_send.at[c, p],
            recv_sem=z_recv.at[c, p],
            device_id=(q, base + p),
            device_id_type=MESH,
        )

    def x_copy(b):
        return pltpu.make_async_remote_copy(
            src_ref=pat.at[0, :, pl.ds(SLAB * b, SLAB)],
            dst_ref=slab.at[pl.ds(BOXES * q, BOXES)],
            send_sem=x_send.at[b],
            recv_sem=x_recv.at[q],
            device_id=(b, r),
            device_id_type=MESH,
        )

    def x_arrival(b):
        return pltpu.make_async_remote_copy(
            src_ref=pat.at[0, :, pl.ds(SLAB * b, SLAB)],
            dst_ref=slab.at[pl.ds(BOXES * b, BOXES)],
            send_sem=x_send.at[b],
            recv_sem=x_recv.at[b],
            device_id=(b, r),
            device_id_type=MESH,
        )

    def a_copy(c):
        target = upper * c + (1 - upper) * (N_BOX - 1 - c)
        return pltpu.make_async_remote_copy(
            src_ref=made.at[c],
            dst_ref=kept.at[q],
            send_sem=a_send.at[c],
            recv_sem=a_recv.at[q],
            device_id=(target, r),
            device_id_type=MESH,
        )

    def meet(p):
        @pl.when(staggered)
        def _():
            pl.semaphore_wait(known.at[p], 1)

    for distance in range(1, OCTET):

        @pl.when((place > distance) | (place == 0))
        def _():
            z_copy(0, jnp.where(place == 0, distance, place - distance)).start()

    for b in range(1, N_BOX):

        @pl.when(b > q)
        def _():
            x_copy(b).start()

    for distance in range(1, OCTET):

        @pl.when((place > 0) & (place + distance < OCTET))
        def _():
            meet(place + distance)
            z_copy(0, place + distance).start()

    for p in range(1, OCTET):

        @pl.when(p != place)
        def _():
            z_copy(1, p).start()

    @pl.when(place > 0)
    def _():
        meet(0)
        z_copy(0, 0).start()
        z_copy(1, 0).start()

    for b in range(N_BOX - 1):

        @pl.when(b < q)
        def _():
            @pl.when(staggered)
            def _():
                pl.semaphore_wait(known_box.at[b], 1)

            x_copy(b).start()

    for c in range(2, CHUNKS):
        for p in range(OCTET):

            @pl.when(p != place)
            def _():
                z_copy(c, p).start()

    interp_tables(high, low)
    phase_tables(lateral, axial)

    def translation():
        for copy in (locals_[0], locals_[1], locals_[2], locals_[4]):
            copy.wait()
        for b in range(N_BOX):

            @pl.when(b != q)
            def _():
                x_arrival(b).wait_recv()


        def one_box(g, carry):
            real = jnp.zeros((SLAB, PHI), F32)
            imag = jnp.zeros((SLAB, PHI), F32)
            for k in range(FAR):
                box, kind = fb[k, g], ft[k, g]
                value = slab[box]
                factor = ops[kind].astype(F32)
                value_r, value_i = value[:, :PHI], value[:, PHI:]
                factor_r, factor_i = factor[:, :PHI], factor[:, PHI:]
                real += factor_r * value_r - factor_i * value_i
                imag += factor_r * value_i + factor_i * value_r
            incoming[0, g, :, 0:PHI] = real
            incoming[0, g, :, PHI : 2 * PHI] = imag
            return carry

        lax.fori_loop(0, GROUP, one_box, 0)

    def refine(c):
        target = upper * c + (1 - upper) * (N_BOX - 1 - c)
        if c in (0, CHUNKS - 1):
            bottom = 1 - upper if c == 0 else upper
            source = pl.multiple_of(8 + bottom * (TH - 8), 8)
            place = pl.multiple_of(bottom * (TH + 8), 8)
            for d in range(OCTET):
                rows = ext[d, pl.ds(source, 8), :]
                ext[d, pl.ds(place, 8), 0:PHI] = pltpu.roll(rows[:, :PHI], PHI // 2, 1)
                ext[d, pl.ds(place, 8), PHI : 2 * PHI] = pltpu.roll(rows[:, PHI:], PHI // 2, 1)
        window = pl.ds(pl.multiple_of(SLAB * target, 8), 2 * SLAB)
        sums = [ext[d, window, :] for d in range(OCTET)]
        for s in (1, 2, 4):
            sums = [sums[k] + sums[k ^ s] if not k & s else sums[k] - sums[k ^ s] for k in range(OCTET)]
        weights = polar_weights(target)
        rows = []
        for k in range(OCTET):
            pieces = jnp.concatenate(halves(sums[k]), axis=0)
            polar = jnp.dot(weights, pieces, preferred_element_type=F32)
            rows += [polar[:, :PHI], polar[:, PHI:]]
        stacked_high, stacked_low = halves(jnp.concatenate(rows, axis=0))
        both = jnp.concatenate([stacked_high, stacked_low], axis=1)
        wide = jnp.dot(both, high[...], preferred_element_type=F32)
        wide += jnp.dot(stacked_high, low[...], preferred_element_type=F32)
        angles = pl.ds(pl.multiple_of(2 * SLAB * target, 8), 2 * SLAB)
        parts = []
        for third in range(2):
            real, imag = 0.0, 0.0
            for k in range(4):
                at = 4 * SLAB * (4 * third + k)
                w_r = wide[at : at + 2 * SLAB]
                w_i = wide[at + 2 * SLAB : at + 4 * SLAB]
                table = lateral[k, angles, :]
                if k == 0:
                    real, imag = table * w_r, table * w_i
                elif k == 3:
                    real, imag = real - table * w_r, imag - table * w_i
                else:
                    real, imag = real - table * w_i, imag + table * w_r
            parts.append((real, imag))
        cosine, sine = axial[0, angles, :], axial[1, angles, :]
        made[c, :, 0 : 2 * PHI] = cosine * parts[0][0] - sine * parts[1][1]
        made[c, :, 2 * PHI : 4 * PHI] = cosine * parts[0][1] + sine * parts[1][0]

        @pl.when(target != q)
        def _():
            a_copy(c).start()

        @pl.when(target == q)
        def _():
            kept[q] = made[c]

    locals_[3].wait()
    for c in range(CHUNKS):
        for p in range(OCTET):

            @pl.when(p != place)
            def _():
                z_arrival(c, p).wait_recv()

        refine(c)
        if c == 1:
            translation()

    for e in range(1, N_BOX):
        other = box_peer(e)
        pltpu.make_async_remote_copy(
            src_ref=made.at[0],
            dst_ref=kept.at[other],
            send_sem=a_send.at[0],
            recv_sem=a_recv.at[other],
            device_id=(other, r),
            device_id_type=MESH,
        ).wait_recv()
    for c in range(CHUNKS):
        target = upper * c + (1 - upper) * (N_BOX - 1 - c)

        @pl.when(target != q)
        def _():
            a_copy(c).wait_send()

        for p in range(OCTET):

            @pl.when(p != place)
            def _():
                z_copy(c, p).wait_send()

    for b in range(N_BOX):

        @pl.when(b != q)
        def _():
            x_copy(b).wait_send()


def shards(patterns, far_boxes, far_types, transfer):
    anywhere = pl.BlockSpec(memory_space=pltpu.HBM)
    vmem = pltpu.VMEM
    dma = pltpu.SemaphoreType.DMA
    return pl.pallas_call(
        kernel,
        out_shape=(
            pltpu.VMEM((1, GROUP, SLAB, 2 * PHI), F32),
            pltpu.VMEM((N_BOX, 2 * SLAB, 4 * PHI), F32),
        ),
        in_specs=[anywhere] * 4,
        out_specs=(pl.BlockSpec(memory_space=vmem),) * 2,
        scratch_shapes=[
            vmem((OCTET, TH + 16, 2 * PHI), F32),
            vmem((GROUP, SLAB, 2 * PHI), F32),
            vmem(transfer.shape, BF16),
            vmem((CHUNKS, 2 * SLAB, 4 * PHI), F32),
            pltpu.SMEM((FAR, GROUP), jnp.int32),
            pltpu.SMEM((FAR, GROUP), jnp.int32),
            vmem((2 * PHI, 2 * PHI), BF16),
            vmem((PHI, 2 * PHI), BF16),
            vmem((4, 2 * TH, 2 * PHI), F32),
            vmem((2, 2 * TH, 2 * PHI), F32),
            pltpu.SemaphoreType.REGULAR((OCTET,)),
            pltpu.SemaphoreType.REGULAR((N_BOX,)),
            dma((CHUNKS, OCTET)),
            dma((CHUNKS, OCTET)),
            dma((N_BOX,)),
            dma((N_BOX,)),
            dma((CHUNKS,)),
            dma((N_BOX,)),
            dma((5,)),
        ],
        compiler_params=pltpu.CompilerParams(
            collective_id=0, has_side_effects=True, vmem_limit_bytes=56 * 1024 * 1024
        ),
    )(patterns, jnp.swapaxes(far_boxes, 1, 2), jnp.swapaxes(far_types, 1, 2), transfer)


def solution(mesh):
    return jax.shard_map(
        shards,
        mesh=mesh,
        in_specs=(
            P("box", "dir", None, None),
            P("dir", None, None),
            P("dir", None, None),
            P(None, "box", None),
        ),
        out_specs=(P("dir", None, "box", None), P("dir", "box", None)),
        check_vma=False,
    )
```

```python
import math

import jax
import jax.numpy as jnp
from jax import lax
from jax.experimental import pallas as pl
from jax.experimental.pallas import tpu as pltpu
from jax.sharding import PartitionSpec as P

MESH = pl.DeviceIdType.MESH
F32, BF16 = jnp.float32, jnp.bfloat16

TH, PHI, BOXES, FAR, GROUP, OCTET, N_BOX = 64, 128, 8, 16, 32, 8, 4
SLAB = TH // N_BOX
CHUNKS = 4
ROWS = (24, 16, 16, 8)
ASCENDING = (0, 24, 40, 56)
DESCENDING = (40, 24, 8, 0)

two_pi = 2.0 * math.pi
step_phase = 8.0
outer_weight = -0.0390625
inner_weight = 0.2734375
center_weight = 0.8203125
across_weight = -0.0546875


def halves(value):
    high = value.astype(BF16)
    return high, (value - high.astype(F32)).astype(BF16)


def index_like(shape, dim):
    return lax.broadcasted_iota(jnp.int32, shape, dim)


def interp_tables(high_ref, low_ref):
    shape = (PHI, 2 * PHI)
    apart = 2 * index_like(shape, 0) - index_like(shape, 1)
    odd = lax.rem(apart + 2 * PHI, 2) == 1
    sign = jnp.where(lax.rem(apart + 2 * PHI, 4) == 1, 1.0, -1.0)
    angle = (math.pi / (2 * PHI)) * apart.astype(F32)
    value = sign * jnp.cos(angle) / (PHI * jnp.where(odd, jnp.sin(angle), 1.0))
    value = jnp.where(odd, value, jnp.where(apart == 0, 1.0, 0.0))
    high, low = halves(value)
    high_ref[0:PHI] = high
    high_ref[PHI : 2 * PHI] = high
    low_ref[...] = low


def phase_tables(lateral, axial):
    shape = (2 * TH, 2 * PHI)
    polar = (math.pi / (2 * TH)) * (index_like(shape, 0).astype(F32) + 0.5)
    azimuth = (two_pi / (2 * PHI)) * index_like(shape, 1).astype(F32)
    sine = step_phase * jnp.sin(polar)
    first, second = sine * jnp.cos(azimuth), sine * jnp.sin(azimuth)
    cos_1, sin_1 = jnp.cos(first), jnp.sin(first)
    cos_2, sin_2 = jnp.cos(second), jnp.sin(second)
    lateral[0] = cos_1 * cos_2
    lateral[1] = sin_1 * cos_2
    lateral[2] = cos_1 * sin_2
    lateral[3] = sin_1 * sin_2
    third = step_phase * jnp.cos(polar)
    axial[0] = jnp.cos(third)
    axial[1] = jnp.sin(third)


def polar_weights(slab):
    shape = (2 * SLAB, 4 * SLAB)
    row, column = index_like(shape, 0), lax.rem(index_like(shape, 1), 2 * SLAB)
    column = jnp.where((slab == 0) & (column < 8), 7 - column, column)
    column = jnp.where((slab == N_BOX - 1) & (column >= 24), 55 - column, column)
    offset = column - 8 - row // 2
    flipped = jnp.where(lax.rem(row, 2) == 0, offset, -offset)
    weights = jnp.zeros(shape, F32)
    for place, weight in ((-2, outer_weight), (-1, inner_weight), (0, center_weight), (1, across_weight)):
        weights = jnp.where(flipped == place, weight, weights)
    return weights.astype(BF16)


def kernel(
    pat, far_boxes, far_types, transfer, incoming, kept,
    ext, slab, ops, made, fb, ft, high, low, lateral, axial,
    known, known_box, z_send, z_recv, x_send, x_recv, a_send, a_recv, local,
):
    q, r = lax.axis_index("box"), lax.axis_index("dir")
    place = lax.rem(r, OCTET)
    base = r - place
    upper, core = q // 2, lax.rem(q, 2)

    def kept_box(p):
        return 4 * lax.rem(p, 2) + 2 * lax.rem(p // 2, 2) + p // 4

    def box_peer(e):
        c = 1 - core if e & 1 else core
        u = 1 - upper if e & 2 else upper
        return 2 * u + c

    def tell(semaphore, p):
        pl.semaphore_signal(semaphore, inc=1, device_id=(q, base + p), device_id_type=MESH)

    barrier = pltpu.get_barrier_semaphore()

    staggered = lax.rem(r // OCTET, 4) < 2
    together = jnp.logical_not(staggered)
    turned = ((q == 0) & (r < OCTET)).astype(jnp.int32)
    latest = (q == 0) & (r == 0)
    rank = lax.rem(place + turned * (OCTET - 1), OCTET)
    ranked = [(p, lax.rem(p + turned * (OCTET - 1), OCTET)) for p in range(OCTET)]

    for p, other in ranked:

        @pl.when((other > rank) | (together & (other < rank)))
        def _():
            tell(barrier, p)

    def tell_box(semaphore, other):
        pl.semaphore_signal(semaphore, inc=1, device_id=(other, r), device_id_type=MESH)

    for b in range(N_BOX):

        @pl.when((b > q) | (together & (b < q)))
        def _():
            tell_box(barrier, b)

    locals_ = [
        pltpu.make_async_copy(far_boxes.at[0], fb, local.at[0]),
        pltpu.make_async_copy(far_types.at[0], ft, local.at[1]),
        pltpu.make_async_copy(transfer, ops, local.at[2]),
        pltpu.make_async_copy(pat.at[0, kept_box(place)], ext.at[place, pl.ds(8, TH)], local.at[3]),
        pltpu.make_async_copy(
            pat.at[0, :, pl.ds(pl.multiple_of(SLAB * q, 8), SLAB)],
            slab.at[pl.ds(BOXES * q, BOXES)],
            local.at[4],
        ),
    ]
    expected = jnp.where(together, OCTET - 1 + N_BOX - 1, rank + q)

    @pl.when(expected > 0)
    def _():
        pl.semaphore_wait(barrier, expected)

    for p, other in ranked:

        @pl.when(staggered & (other < rank))
        def _():
            tell(known.at[place], p)

    for b in range(N_BOX - 1):

        @pl.when(staggered & (b < q))
        def _():
            tell_box(known_box.at[q], b)

    def z_copy(c, p):
        first = pl.multiple_of(upper * ASCENDING[c] + (1 - upper) * DESCENDING[c], 8)
        return pltpu.make_async_remote_copy(
            src_ref=pat.at[0, kept_box(p), pl.ds(first, ROWS[c])],
            dst_ref=ext.at[place, pl.ds(pl.multiple_of(8 + first, 8), ROWS[c])],
            send_sem=z_send.at[c, p],
            recv_sem=z_recv.at[c, place],
            device_id=(q, base + p),
            device_id_type=MESH,
        )

    def z_arrival(c, p):
        first = pl.multiple_of(upper * ASCENDING[c] + (1 - upper) * DESCENDING[c], 8)
        return pltpu.make_async_remote_copy(
            src_ref=pat.at[0, 0, pl.ds(first, ROWS[c])],
            dst_ref=ext.at[p, pl.ds(pl.multiple_of(8 + first, 8), ROWS[c])],
            send_sem=z_send.at[c, p],
            recv_sem=z_recv.at[c, p],
            device_id=(q, base + p),
            device_id_type=MESH,
        )

    def x_copy(b):
        return pltpu.make_async_remote_copy(
            src_ref=pat.at[0, :, pl.ds(SLAB * b, SLAB)],
            dst_ref=slab.at[pl.ds(BOXES * q, BOXES)],
            send_sem=x_send.at[b],
            recv_sem=x_recv.at[q],
            device_id=(b, r),
            device_id_type=MESH,
        )

    def x_arrival(b):
        return pltpu.make_async_remote_copy(
            src_ref=pat.at[0, :, pl.ds(SLAB * b, SLAB)],
            dst_ref=slab.at[pl.ds(BOXES * b, BOXES)],
            send_sem=x_send.at[b],
            recv_sem=x_recv.at[b],
            device_id=(b, r),
            device_id_type=MESH,
        )

    def a_copy(c):
        target = upper * c + (1 - upper) * (N_BOX - 1 - c)
        return pltpu.make_async_remote_copy(
            src_ref=made.at[c],
            dst_ref=kept.at[q],
            send_sem=a_send.at[c],
            recv_sem=a_recv.at[q],
            device_id=(target, r),
            device_id_type=MESH,
        )

    def meet(p):
        @pl.when(staggered)
        def _():
            pl.semaphore_wait(known.at[p], 1)

    for distance in range(1, OCTET):
        lower = rank >= distance

        @pl.when(lower)
        def _():
            z_copy(0, lax.rem(rank - distance + turned, OCTET)).start()

    for copy in locals_:
        copy.start()

    for b in range(N_BOX - 1):

        @pl.when(b < q)
        def _():
            x_copy(b).start()

    for distance in range(1, OCTET):
        higher = rank + distance < OCTET - turned

        @pl.when(higher)
        def _():
            meet(place + distance)
            z_copy(0, place + distance).start()

    for b in range(1, N_BOX):

        @pl.when(b > q)
        def _():
            @pl.when(staggered)
            def _():
                pl.semaphore_wait(known_box.at[b], 1)

            x_copy(b).start()

    for p in range(OCTET):

        @pl.when((p != place) & ((p > 0) | (turned == 0) | (place == 0)))
        def _():
            z_copy(1, p).start()

    @pl.when((turned == 1) & (place > 0))
    def _():
        meet(0)
        for c in range(2):
            z_copy(c, 0).start()

    @pl.when(together)
    def _():
        for c in range(2, CHUNKS):
            for p in range(OCTET):

                @pl.when(p != place)
                def _():
                    z_copy(c, p).start()

    @pl.when(staggered)
    def _():
        for p in range(OCTET):

            @pl.when(p != place)
            def _():
                for c in range(2, CHUNKS):
                    z_copy(c, p).start()

    interp_tables(high, low)
    phase_tables(lateral, axial)

    def translation():
        for copy in (locals_[0], locals_[1], locals_[2], locals_[4]):
            copy.wait()
        for b in range(N_BOX):

            @pl.when(b != q)
            def _():
                x_arrival(b).wait_recv()


        def one_box(g, carry):
            real = jnp.zeros((SLAB, PHI), F32)
            imag = jnp.zeros((SLAB, PHI), F32)
            for k in range(FAR):
                box, kind = fb[k, g], ft[k, g]
                value = slab[box]
                factor = ops[kind].astype(F32)
                value_r, value_i = value[:, :PHI], value[:, PHI:]
                factor_r, factor_i = factor[:, :PHI], factor[:, PHI:]
                real += factor_r * value_r - factor_i * value_i
                imag += factor_r * value_i + factor_i * value_r
            incoming[0, g, :, 0:PHI] = real
            incoming[0, g, :, PHI : 2 * PHI] = imag
            return carry

        lax.fori_loop(0, GROUP, one_box, 0)

    def refine(c):
        target = upper * c + (1 - upper) * (N_BOX - 1 - c)
        if c in (0, CHUNKS - 1):
            bottom = 1 - upper if c == 0 else upper
            source = pl.multiple_of(8 + bottom * (TH - 8), 8)
            place = pl.multiple_of(bottom * (TH + 8), 8)
            for d in range(OCTET):
                rows = ext[d, pl.ds(source, 8), :]
                ext[d, pl.ds(place, 8), 0:PHI] = pltpu.roll(rows[:, :PHI], PHI // 2, 1)
                ext[d, pl.ds(place, 8), PHI : 2 * PHI] = pltpu.roll(rows[:, PHI:], PHI // 2, 1)
        window = pl.ds(pl.multiple_of(SLAB * target, 8), 2 * SLAB)
        sums = [ext[d, window, :] for d in range(OCTET)]
        for s in (1, 2, 4):
            sums = [sums[k] + sums[k ^ s] if not k & s else sums[k] - sums[k ^ s] for k in range(OCTET)]
        weights = polar_weights(target)
        rows = []
        for k in range(OCTET):
            pieces = jnp.concatenate(halves(sums[k]), axis=0)
            polar = jnp.dot(weights, pieces, preferred_element_type=F32)
            rows += [polar[:, :PHI], polar[:, PHI:]]
        stacked_high, stacked_low = halves(jnp.concatenate(rows, axis=0))
        both = jnp.concatenate([stacked_high, stacked_low], axis=1)
        wide = jnp.dot(both, high[...], preferred_element_type=F32)
        wide += jnp.dot(stacked_high, low[...], preferred_element_type=F32)
        angles = pl.ds(pl.multiple_of(2 * SLAB * target, 8), 2 * SLAB)
        parts = []
        for third in range(2):
            real, imag = 0.0, 0.0
            for k in range(4):
                at = 4 * SLAB * (4 * third + k)
                w_r = wide[at : at + 2 * SLAB]
                w_i = wide[at + 2 * SLAB : at + 4 * SLAB]
                table = lateral[k, angles, :]
                if k == 0:
                    real, imag = table * w_r, table * w_i
                elif k == 3:
                    real, imag = real - table * w_r, imag - table * w_i
                else:
                    real, imag = real - table * w_i, imag + table * w_r
            parts.append((real, imag))
        cosine, sine = axial[0, angles, :], axial[1, angles, :]
        made[c, :, 0 : 2 * PHI] = cosine * parts[0][0] - sine * parts[1][1]
        made[c, :, 2 * PHI : 4 * PHI] = cosine * parts[0][1] + sine * parts[1][0]

        @pl.when(target != q)
        def _():
            a_copy(c).start()

        @pl.when(target == q)
        def _():
            kept[q] = made[c]

    locals_[3].wait()
    for c in range(CHUNKS):
        for p in range(OCTET):

            @pl.when(p != place)
            def _():
                z_arrival(c, p).wait_recv()

        refine(c)
        if c == 1:

            @pl.when(jnp.logical_not(latest))
            def _():
                translation()

    @pl.when(latest)
    def _():
        translation()

    for e in range(1, N_BOX):
        other = box_peer(e)
        pltpu.make_async_remote_copy(
            src_ref=made.at[0],
            dst_ref=kept.at[other],
            send_sem=a_send.at[0],
            recv_sem=a_recv.at[other],
            device_id=(other, r),
            device_id_type=MESH,
        ).wait_recv()
    for c in range(CHUNKS):
        target = upper * c + (1 - upper) * (N_BOX - 1 - c)

        @pl.when(target != q)
        def _():
            a_copy(c).wait_send()

        for p in range(OCTET):

            @pl.when(p != place)
            def _():
                z_copy(c, p).wait_send()

    for b in range(N_BOX):

        @pl.when(b != q)
        def _():
            x_copy(b).wait_send()


def shards(patterns, far_boxes, far_types, transfer):
    anywhere = pl.BlockSpec(memory_space=pltpu.HBM)
    vmem = pltpu.VMEM
    dma = pltpu.SemaphoreType.DMA
    return pl.pallas_call(
        kernel,
        out_shape=(
            pltpu.VMEM((1, GROUP, SLAB, 2 * PHI), F32),
            pltpu.VMEM((N_BOX, 2 * SLAB, 4 * PHI), F32),
        ),
        in_specs=[anywhere] * 4,
        out_specs=(pl.BlockSpec(memory_space=vmem),) * 2,
        scratch_shapes=[
            vmem((OCTET, TH + 16, 2 * PHI), F32),
            vmem((GROUP, SLAB, 2 * PHI), F32),
            vmem(transfer.shape, BF16),
            vmem((CHUNKS, 2 * SLAB, 4 * PHI), F32),
            pltpu.SMEM((FAR, GROUP), jnp.int32),
            pltpu.SMEM((FAR, GROUP), jnp.int32),
            vmem((2 * PHI, 2 * PHI), BF16),
            vmem((PHI, 2 * PHI), BF16),
            vmem((4, 2 * TH, 2 * PHI), F32),
            vmem((2, 2 * TH, 2 * PHI), F32),
            pltpu.SemaphoreType.REGULAR((OCTET,)),
            pltpu.SemaphoreType.REGULAR((N_BOX,)),
            dma((CHUNKS, OCTET)),
            dma((CHUNKS, OCTET)),
            dma((N_BOX,)),
            dma((N_BOX,)),
            dma((CHUNKS,)),
            dma((N_BOX,)),
            dma((5,)),
        ],
        compiler_params=pltpu.CompilerParams(
            collective_id=0, has_side_effects=True, vmem_limit_bytes=56 * 1024 * 1024
        ),
    )(patterns, jnp.swapaxes(far_boxes, 1, 2), jnp.swapaxes(far_types, 1, 2), transfer)


def solution(mesh):
    return jax.shard_map(
        shards,
        mesh=mesh,
        in_specs=(
            P("box", "dir", None, None),
            P("dir", None, None),
            P("dir", None, None),
            P(None, "box", None),
        ),
        out_specs=(P("dir", None, "box", None), P("dir", "box", None)),
        check_vma=False,
    )
```

```python
import math

import jax
import jax.numpy as jnp
from jax import lax
from jax.experimental import pallas as pl
from jax.experimental.pallas import tpu as pltpu
from jax.sharding import PartitionSpec as P

MESH = pl.DeviceIdType.MESH
F32, BF16 = jnp.float32, jnp.bfloat16

TH, PHI, BOXES, FAR, GROUP, OCTET, N_BOX = 64, 128, 8, 16, 32, 8, 4
SLAB = TH // N_BOX
CHUNKS = 4
ROWS = (24, 16, 16, 8)
ASCENDING = (0, 24, 40, 56)
DESCENDING = (40, 24, 8, 0)

two_pi = 2.0 * math.pi
step_phase = 8.0
outer_weight = -0.0390625
inner_weight = 0.2734375
center_weight = 0.8203125
across_weight = -0.0546875


def halves(value):
    high = value.astype(BF16)
    return high, (value - high.astype(F32)).astype(BF16)


def index_like(shape, dim):
    return lax.broadcasted_iota(jnp.int32, shape, dim)


def interp_tables(high_ref, low_ref):
    shape = (PHI, 2 * PHI)
    apart = 2 * index_like(shape, 0) - index_like(shape, 1)
    odd = lax.rem(apart + 2 * PHI, 2) == 1
    sign = jnp.where(lax.rem(apart + 2 * PHI, 4) == 1, 1.0, -1.0)
    angle = (math.pi / (2 * PHI)) * apart.astype(F32)
    value = sign * jnp.cos(angle) / (PHI * jnp.where(odd, jnp.sin(angle), 1.0))
    value = jnp.where(odd, value, jnp.where(apart == 0, 1.0, 0.0))
    high, low = halves(value)
    high_ref[0:PHI] = high
    high_ref[PHI : 2 * PHI] = high
    low_ref[...] = low


def phase_tables(lateral, axial):
    shape = (2 * TH, 2 * PHI)
    polar = (math.pi / (2 * TH)) * (index_like(shape, 0).astype(F32) + 0.5)
    azimuth = (two_pi / (2 * PHI)) * index_like(shape, 1).astype(F32)
    sine = step_phase * jnp.sin(polar)
    first, second = sine * jnp.cos(azimuth), sine * jnp.sin(azimuth)
    cos_1, sin_1 = jnp.cos(first), jnp.sin(first)
    cos_2, sin_2 = jnp.cos(second), jnp.sin(second)
    lateral[0] = cos_1 * cos_2
    lateral[1] = sin_1 * cos_2
    lateral[2] = cos_1 * sin_2
    lateral[3] = sin_1 * sin_2
    third = step_phase * jnp.cos(polar)
    axial[0] = jnp.cos(third)
    axial[1] = jnp.sin(third)


def polar_weights(slab):
    shape = (2 * SLAB, 4 * SLAB)
    row, column = index_like(shape, 0), lax.rem(index_like(shape, 1), 2 * SLAB)
    column = jnp.where((slab == 0) & (column < 8), 7 - column, column)
    column = jnp.where((slab == N_BOX - 1) & (column >= 24), 55 - column, column)
    offset = column - 8 - row // 2
    flipped = jnp.where(lax.rem(row, 2) == 0, offset, -offset)
    weights = jnp.zeros(shape, F32)
    for place, weight in ((-2, outer_weight), (-1, inner_weight), (0, center_weight), (1, across_weight)):
        weights = jnp.where(flipped == place, weight, weights)
    return weights.astype(BF16)


def kernel(
    pat, far_boxes, far_types, transfer, incoming, kept,
    ext, slab, ops, made, fb, ft, high, low, lateral, axial,
    known, known_box, z_send, z_recv, x_send, x_recv, a_send, a_recv, local,
):
    q, r = lax.axis_index("box"), lax.axis_index("dir")
    place = lax.rem(r, OCTET)
    base = r - place
    upper, core = q // 2, lax.rem(q, 2)

    def kept_box(p):
        return 4 * lax.rem(p, 2) + 2 * lax.rem(p // 2, 2) + p // 4

    def box_peer(e):
        c = 1 - core if e & 1 else core
        u = 1 - upper if e & 2 else upper
        return 2 * u + c

    def tell(semaphore, p):
        pl.semaphore_signal(semaphore, inc=1, device_id=(q, base + p), device_id_type=MESH)

    barrier = pltpu.get_barrier_semaphore()

    staggered = lax.rem(r // OCTET, 4) < 2
    together = jnp.logical_not(staggered)
    turned = ((q == 0) & (r < OCTET)).astype(jnp.int32)
    latest = (q == 0) & (r == 0)
    rank = lax.rem(place + turned * (OCTET - 1), OCTET)
    ranked = [(p, lax.rem(p + turned * (OCTET - 1), OCTET)) for p in range(OCTET)]

    for p, other in ranked:

        @pl.when((other > rank) | (together & (other < rank)))
        def _():
            tell(barrier, p)

    def tell_box(semaphore, other):
        pl.semaphore_signal(semaphore, inc=1, device_id=(other, r), device_id_type=MESH)

    for b in range(N_BOX):

        @pl.when((b > q) | (together & (b < q)))
        def _():
            tell_box(barrier, b)

    locals_ = [
        pltpu.make_async_copy(far_boxes.at[0], fb, local.at[0]),
        pltpu.make_async_copy(far_types.at[0], ft, local.at[1]),
        pltpu.make_async_copy(transfer, ops, local.at[2]),
        pltpu.make_async_copy(pat.at[0, kept_box(place)], ext.at[place, pl.ds(8, TH)], local.at[3]),
        pltpu.make_async_copy(
            pat.at[0, :, pl.ds(pl.multiple_of(SLAB * q, 8), SLAB)],
            slab.at[pl.ds(BOXES * q, BOXES)],
            local.at[4],
        ),
    ]
    expected = jnp.where(together, OCTET - 1 + N_BOX - 1, rank + q)

    @pl.when(expected > 0)
    def _():
        pl.semaphore_wait(barrier, expected)

    for p, other in ranked:

        @pl.when(staggered & (other < rank))
        def _():
            tell(known.at[place], p)

    for b in range(N_BOX - 1):

        @pl.when(staggered & (b < q))
        def _():
            tell_box(known_box.at[q], b)

    def z_copy(c, p):
        first = pl.multiple_of(upper * ASCENDING[c] + (1 - upper) * DESCENDING[c], 8)
        return pltpu.make_async_remote_copy(
            src_ref=pat.at[0, kept_box(p), pl.ds(first, ROWS[c])],
            dst_ref=ext.at[place, pl.ds(pl.multiple_of(8 + first, 8), ROWS[c])],
            send_sem=z_send.at[c, p],
            recv_sem=z_recv.at[c, place],
            device_id=(q, base + p),
            device_id_type=MESH,
        )

    def z_arrival(c, p):
        first = pl.multiple_of(upper * ASCENDING[c] + (1 - upper) * DESCENDING[c], 8)
        return pltpu.make_async_remote_copy(
            src_ref=pat.at[0, 0, pl.ds(first, ROWS[c])],
            dst_ref=ext.at[p, pl.ds(pl.multiple_of(8 + first, 8), ROWS[c])],
            send_sem=z_send.at[c, p],
            recv_sem=z_recv.at[c, p],
            device_id=(q, base + p),
            device_id_type=MESH,
        )

    def x_copy(b):
        return pltpu.make_async_remote_copy(
            src_ref=pat.at[0, :, pl.ds(SLAB * b, SLAB)],
            dst_ref=slab.at[pl.ds(BOXES * q, BOXES)],
            send_sem=x_send.at[b],
            recv_sem=x_recv.at[q],
            device_id=(b, r),
            device_id_type=MESH,
        )

    def x_arrival(b):
        return pltpu.make_async_remote_copy(
            src_ref=pat.at[0, :, pl.ds(SLAB * b, SLAB)],
            dst_ref=slab.at[pl.ds(BOXES * b, BOXES)],
            send_sem=x_send.at[b],
            recv_sem=x_recv.at[b],
            device_id=(b, r),
            device_id_type=MESH,
        )

    def a_copy(c):
        target = upper * c + (1 - upper) * (N_BOX - 1 - c)
        return pltpu.make_async_remote_copy(
            src_ref=made.at[c],
            dst_ref=kept.at[q],
            send_sem=a_send.at[c],
            recv_sem=a_recv.at[q],
            device_id=(target, r),
            device_id_type=MESH,
        )

    def meet(p):
        @pl.when(staggered)
        def _():
            pl.semaphore_wait(known.at[p], 1)

    for distance in range(1, OCTET):
        lower = rank >= distance

        @pl.when(lower)
        def _():
            z_copy(0, lax.rem(rank - distance + turned, OCTET)).start()

    for copy in locals_:
        copy.start()

    for b in range(N_BOX - 1):

        @pl.when(b < q)
        def _():
            x_copy(b).start()

    for distance in range(1, OCTET):
        higher = rank + distance < OCTET - turned

        @pl.when(higher)
        def _():
            meet(place + distance)
            z_copy(0, place + distance).start()

    for b in range(1, N_BOX):

        @pl.when(b > q)
        def _():
            @pl.when(staggered)
            def _():
                pl.semaphore_wait(known_box.at[b], 1)

            x_copy(b).start()

    for p in range(OCTET):

        @pl.when((p != place) & ((p > 0) | (turned == 0) | (place == 0)))
        def _():
            z_copy(1, p).start()

    @pl.when((turned == 1) & (place > 0))
    def _():
        meet(0)
        for c in range(2):
            z_copy(c, 0).start()

    @pl.when(together)
    def _():
        for c in range(2, CHUNKS):
            for p in range(OCTET):

                @pl.when(p != place)
                def _():
                    z_copy(c, p).start()

    @pl.when(staggered)
    def _():
        for p in range(OCTET):

            @pl.when(p != place)
            def _():
                for c in range(2, CHUNKS):
                    z_copy(c, p).start()

    interp_tables(high, low)
    phase_tables(lateral, axial)

    def translation():
        for copy in (locals_[0], locals_[1], locals_[2], locals_[4]):
            copy.wait()
        for b in range(N_BOX):

            @pl.when(b != q)
            def _():
                x_arrival(b).wait_recv()


        def one_box(g, carry):
            real = jnp.zeros((SLAB, PHI), F32)
            imag = jnp.zeros((SLAB, PHI), F32)
            for k in range(FAR):
                box, kind = fb[k, g], ft[k, g]
                value = slab[box]
                factor = ops[kind].astype(F32)
                value_r, value_i = value[:, :PHI], value[:, PHI:]
                factor_r, factor_i = factor[:, :PHI], factor[:, PHI:]
                real += factor_r * value_r - factor_i * value_i
                imag += factor_r * value_i + factor_i * value_r
            incoming[0, g, :, 0:PHI] = real
            incoming[0, g, :, PHI : 2 * PHI] = imag
            return carry

        lax.fori_loop(0, GROUP, one_box, 0)

    def refine(c):
        target = upper * c + (1 - upper) * (N_BOX - 1 - c)
        if c in (0, CHUNKS - 1):
            bottom = 1 - upper if c == 0 else upper
            source = pl.multiple_of(8 + bottom * (TH - 8), 8)
            place = pl.multiple_of(bottom * (TH + 8), 8)
            for d in range(OCTET):
                rows = ext[d, pl.ds(source, 8), :]
                ext[d, pl.ds(place, 8), 0:PHI] = pltpu.roll(rows[:, :PHI], PHI // 2, 1)
                ext[d, pl.ds(place, 8), PHI : 2 * PHI] = pltpu.roll(rows[:, PHI:], PHI // 2, 1)
        window = pl.ds(pl.multiple_of(SLAB * target, 8), 2 * SLAB)
        sums = [ext[d, window, :] for d in range(OCTET)]
        for s in (1, 2, 4):
            sums = [sums[k] + sums[k ^ s] if not k & s else sums[k] - sums[k ^ s] for k in range(OCTET)]
        weights = polar_weights(target)
        rows = []
        for k in range(OCTET):
            pieces = jnp.concatenate(halves(sums[k]), axis=0)
            polar = jnp.dot(weights, pieces, preferred_element_type=F32)
            rows += [polar[:, :PHI], polar[:, PHI:]]
        stacked_high, stacked_low = halves(jnp.concatenate(rows, axis=0))
        both = jnp.concatenate([stacked_high, stacked_low], axis=1)
        wide = jnp.dot(both, high[...], preferred_element_type=F32)
        wide += jnp.dot(stacked_high, low[...], preferred_element_type=F32)
        angles = pl.ds(pl.multiple_of(2 * SLAB * target, 8), 2 * SLAB)
        parts = []
        for third in range(2):
            real, imag = 0.0, 0.0
            for k in range(4):
                at = 4 * SLAB * (4 * third + k)
                w_r = wide[at : at + 2 * SLAB]
                w_i = wide[at + 2 * SLAB : at + 4 * SLAB]
                table = lateral[k, angles, :]
                if k == 0:
                    real, imag = table * w_r, table * w_i
                elif k == 3:
                    real, imag = real - table * w_r, imag - table * w_i
                else:
                    real, imag = real - table * w_i, imag + table * w_r
            parts.append((real, imag))
        cosine, sine = axial[0, angles, :], axial[1, angles, :]
        made[c, :, 0 : 2 * PHI] = cosine * parts[0][0] - sine * parts[1][1]
        made[c, :, 2 * PHI : 4 * PHI] = cosine * parts[0][1] + sine * parts[1][0]

        @pl.when(target != q)
        def _():
            a_copy(c).start()

        @pl.when(target == q)
        def _():
            kept[q] = made[c]

    locals_[3].wait()
    for c in range(CHUNKS):
        for p in range(OCTET):

            @pl.when(p != place)
            def _():
                z_arrival(c, p).wait_recv()

        refine(c)
        if c == 1:

            @pl.when(jnp.logical_not(latest))
            def _():
                translation()

    @pl.when(latest)
    def _():
        translation()

    for e in range(1, N_BOX):
        other = box_peer(e)
        pltpu.make_async_remote_copy(
            src_ref=made.at[0],
            dst_ref=kept.at[other],
            send_sem=a_send.at[0],
            recv_sem=a_recv.at[other],
            device_id=(other, r),
            device_id_type=MESH,
        ).wait_recv()
    for c in range(CHUNKS):
        target = upper * c + (1 - upper) * (N_BOX - 1 - c)

        @pl.when(target != q)
        def _():
            a_copy(c).wait_send()

        for p in range(OCTET):

            @pl.when(p != place)
            def _():
                z_copy(c, p).wait_send()

    for b in range(N_BOX):

        @pl.when(b != q)
        def _():
            x_copy(b).wait_send()


def finish(made_inc, made_agg, incoming, aggregated, sems):
    copies = [
        pltpu.make_async_copy(made_inc, incoming, sems.at[0]),
        pltpu.make_async_copy(made_agg, aggregated, sems.at[1]),
    ]
    for copy in copies:
        copy.start()
    for copy in copies:
        copy.wait()


def shards(patterns, far_boxes, far_types, transfer):
    anywhere = pl.BlockSpec(memory_space=pltpu.HBM)
    vmem = pltpu.VMEM
    dma = pltpu.SemaphoreType.DMA
    results = pl.pallas_call(
        kernel,
        out_shape=(
            pltpu.VMEM((1, GROUP, SLAB, 2 * PHI), F32),
            pltpu.VMEM((N_BOX, 2 * SLAB, 4 * PHI), F32),
        ),
        in_specs=[anywhere] * 4,
        out_specs=(pl.BlockSpec(memory_space=vmem),) * 2,
        scratch_shapes=[
            vmem((OCTET, TH + 16, 2 * PHI), F32),
            vmem((GROUP, SLAB, 2 * PHI), F32),
            vmem(transfer.shape, BF16),
            vmem((CHUNKS, 2 * SLAB, 4 * PHI), F32),
            pltpu.SMEM((FAR, GROUP), jnp.int32),
            pltpu.SMEM((FAR, GROUP), jnp.int32),
            vmem((2 * PHI, 2 * PHI), BF16),
            vmem((PHI, 2 * PHI), BF16),
            vmem((4, 2 * TH, 2 * PHI), F32),
            vmem((2, 2 * TH, 2 * PHI), F32),
            pltpu.SemaphoreType.REGULAR((OCTET,)),
            pltpu.SemaphoreType.REGULAR((N_BOX,)),
            dma((CHUNKS, OCTET)),
            dma((CHUNKS, OCTET)),
            dma((N_BOX,)),
            dma((N_BOX,)),
            dma((CHUNKS,)),
            dma((N_BOX,)),
            dma((5,)),
        ],
        compiler_params=pltpu.CompilerParams(
            collective_id=0, has_side_effects=True, vmem_limit_bytes=56 * 1024 * 1024
        ),
    )(patterns, jnp.swapaxes(far_boxes, 1, 2), jnp.swapaxes(far_types, 1, 2), transfer)
    return pl.pallas_call(
        finish,
        out_shape=tuple(pltpu.HBM(v.shape, v.dtype) for v in results),
        in_specs=[pl.BlockSpec(memory_space=pl.ANY)] * 2,
        out_specs=(pl.BlockSpec(memory_space=pl.ANY),) * 2,
        scratch_shapes=[dma((2,))],
        compiler_params=pltpu.CompilerParams(vmem_limit_bytes=1024 * 1024),
    )(*results)


def solution(mesh):
    return jax.shard_map(
        shards,
        mesh=mesh,
        in_specs=(
            P("box", "dir", None, None),
            P("dir", None, None),
            P("dir", None, None),
            P(None, "box", None),
        ),
        out_specs=(P("dir", None, "box", None), P("dir", "box", None)),
        check_vma=False,
    )
```

```python
import math

import jax
import jax.numpy as jnp
from jax import lax
from jax.experimental import pallas as pl
from jax.experimental.pallas import tpu as pltpu
from jax.sharding import PartitionSpec as P

MESH = pl.DeviceIdType.MESH
F32, BF16 = jnp.float32, jnp.bfloat16

TH, PHI, BOXES, FAR, GROUP, OCTET, N_BOX = 64, 128, 8, 16, 32, 8, 4
SLAB = TH // N_BOX
CHUNKS = 4
ROWS = (24, 16, 16, 8)
ASCENDING = (0, 24, 40, 56)
DESCENDING = (40, 24, 8, 0)

two_pi = 2.0 * math.pi
step_phase = 8.0
outer_weight = -0.0390625
inner_weight = 0.2734375
center_weight = 0.8203125
across_weight = -0.0546875


def halves(value):
    high = value.astype(BF16)
    return high, (value - high.astype(F32)).astype(BF16)


def index_like(shape, dim):
    return lax.broadcasted_iota(jnp.int32, shape, dim)


def interp_tables(high_ref, low_ref):
    shape = (PHI, 2 * PHI)
    apart = 2 * index_like(shape, 0) - index_like(shape, 1)
    odd = lax.rem(apart + 2 * PHI, 2) == 1
    sign = jnp.where(lax.rem(apart + 2 * PHI, 4) == 1, 1.0, -1.0)
    angle = (math.pi / (2 * PHI)) * apart.astype(F32)
    value = sign * jnp.cos(angle) / (PHI * jnp.where(odd, jnp.sin(angle), 1.0))
    value = jnp.where(odd, value, jnp.where(apart == 0, 1.0, 0.0))
    high, low = halves(value)
    high_ref[0:PHI] = high
    high_ref[PHI : 2 * PHI] = high
    low_ref[...] = low


def phase_tables(lateral, axial):
    shape = (2 * TH, 2 * PHI)
    polar = (math.pi / (2 * TH)) * (index_like(shape, 0).astype(F32) + 0.5)
    azimuth = (two_pi / (2 * PHI)) * index_like(shape, 1).astype(F32)
    sine = step_phase * jnp.sin(polar)
    first, second = sine * jnp.cos(azimuth), sine * jnp.sin(azimuth)
    cos_1, sin_1 = jnp.cos(first), jnp.sin(first)
    cos_2, sin_2 = jnp.cos(second), jnp.sin(second)
    lateral[0] = cos_1 * cos_2
    lateral[1] = sin_1 * cos_2
    lateral[2] = cos_1 * sin_2
    lateral[3] = sin_1 * sin_2
    third = step_phase * jnp.cos(polar)
    axial[0] = jnp.cos(third)
    axial[1] = jnp.sin(third)


def polar_weights(slab):
    shape = (2 * SLAB, 4 * SLAB)
    row, column = index_like(shape, 0), lax.rem(index_like(shape, 1), 2 * SLAB)
    column = jnp.where((slab == 0) & (column < 8), 7 - column, column)
    column = jnp.where((slab == N_BOX - 1) & (column >= 24), 55 - column, column)
    offset = column - 8 - row // 2
    flipped = jnp.where(lax.rem(row, 2) == 0, offset, -offset)
    weights = jnp.zeros(shape, F32)
    for place, weight in ((-2, outer_weight), (-1, inner_weight), (0, center_weight), (1, across_weight)):
        weights = jnp.where(flipped == place, weight, weights)
    return weights.astype(BF16)


def kernel(
    pat, far_boxes, far_types, transfer, incoming, kept,
    ext, slab, ops, made, fb, ft, high, low, lateral, axial,
    known, known_box, z_send, z_recv, x_send, x_recv, a_send, a_recv, local,
):
    q, r = lax.axis_index("box"), lax.axis_index("dir")
    place = lax.rem(r, OCTET)
    base = r - place
    upper, core = q // 2, lax.rem(q, 2)

    def kept_box(p):
        return 4 * lax.rem(p, 2) + 2 * lax.rem(p // 2, 2) + p // 4

    def box_peer(e):
        c = 1 - core if e & 1 else core
        u = 1 - upper if e & 2 else upper
        return 2 * u + c

    def tell(semaphore, p):
        pl.semaphore_signal(semaphore, inc=1, device_id=(q, base + p), device_id_type=MESH)

    barrier = pltpu.get_barrier_semaphore()

    staggered = lax.rem(r // OCTET, 4) < 2
    together = jnp.logical_not(staggered)
    turned = ((q == 0) & (r < OCTET)).astype(jnp.int32)
    latest = (q == 0) & (r == 0)
    rank = lax.rem(place + turned * (OCTET - 1), OCTET)
    ranked = [(p, lax.rem(p + turned * (OCTET - 1), OCTET)) for p in range(OCTET)]

    for p, other in ranked:

        @pl.when((other > rank) | (together & (other < rank)))
        def _():
            tell(barrier, p)

    def tell_box(semaphore, other):
        pl.semaphore_signal(semaphore, inc=1, device_id=(other, r), device_id_type=MESH)

    for b in range(N_BOX):

        @pl.when((b > q) | (together & (b < q)))
        def _():
            tell_box(barrier, b)

    locals_ = [
        pltpu.make_async_copy(far_boxes.at[0], fb, local.at[0]),
        pltpu.make_async_copy(far_types.at[0], ft, local.at[1]),
        pltpu.make_async_copy(transfer, ops, local.at[2]),
        pltpu.make_async_copy(pat.at[0, kept_box(place)], ext.at[place, pl.ds(8, TH)], local.at[3]),
        pltpu.make_async_copy(
            pat.at[0, :, pl.ds(pl.multiple_of(SLAB * q, 8), SLAB)],
            slab.at[pl.ds(BOXES * q, BOXES)],
            local.at[4],
        ),
    ]
    expected = jnp.where(together, OCTET - 1 + N_BOX - 1, rank + q)

    @pl.when(expected > 0)
    def _():
        pl.semaphore_wait(barrier, expected)

    for p, other in ranked:

        @pl.when(staggered & (other < rank))
        def _():
            tell(known.at[place], p)

    for b in range(N_BOX - 1):

        @pl.when(staggered & (b < q))
        def _():
            tell_box(known_box.at[q], b)

    def z_copy(c, p):
        first = pl.multiple_of(upper * ASCENDING[c] + (1 - upper) * DESCENDING[c], 8)
        return pltpu.make_async_remote_copy(
            src_ref=pat.at[0, kept_box(p), pl.ds(first, ROWS[c])],
            dst_ref=ext.at[place, pl.ds(pl.multiple_of(8 + first, 8), ROWS[c])],
            send_sem=z_send.at[c, p],
            recv_sem=z_recv.at[c, place],
            device_id=(q, base + p),
            device_id_type=MESH,
        )

    def z_arrival(c, p):
        first = pl.multiple_of(upper * ASCENDING[c] + (1 - upper) * DESCENDING[c], 8)
        return pltpu.make_async_remote_copy(
            src_ref=pat.at[0, 0, pl.ds(first, ROWS[c])],
            dst_ref=ext.at[p, pl.ds(pl.multiple_of(8 + first, 8), ROWS[c])],
            send_sem=z_send.at[c, p],
            recv_sem=z_recv.at[c, p],
            device_id=(q, base + p),
            device_id_type=MESH,
        )

    def x_copy(b):
        return pltpu.make_async_remote_copy(
            src_ref=pat.at[0, :, pl.ds(SLAB * b, SLAB)],
            dst_ref=slab.at[pl.ds(BOXES * q, BOXES)],
            send_sem=x_send.at[b],
            recv_sem=x_recv.at[q],
            device_id=(b, r),
            device_id_type=MESH,
        )

    def x_arrival(b):
        return pltpu.make_async_remote_copy(
            src_ref=pat.at[0, :, pl.ds(SLAB * b, SLAB)],
            dst_ref=slab.at[pl.ds(BOXES * b, BOXES)],
            send_sem=x_send.at[b],
            recv_sem=x_recv.at[b],
            device_id=(b, r),
            device_id_type=MESH,
        )

    def a_copy(c):
        target = upper * c + (1 - upper) * (N_BOX - 1 - c)
        return pltpu.make_async_remote_copy(
            src_ref=made.at[c],
            dst_ref=kept.at[q],
            send_sem=a_send.at[c],
            recv_sem=a_recv.at[q],
            device_id=(target, r),
            device_id_type=MESH,
        )

    def meet(p):
        @pl.when(staggered)
        def _():
            pl.semaphore_wait(known.at[p], 1)

    for distance in range(1, OCTET):
        lower = rank >= distance

        @pl.when(lower)
        def _():
            z_copy(0, lax.rem(rank - distance + turned, OCTET)).start()

    for copy in locals_:
        copy.start()

    for b in range(N_BOX - 1):

        @pl.when(b < q)
        def _():
            x_copy(b).start()

    for distance in range(1, OCTET):
        higher = rank + distance < OCTET - turned

        @pl.when(higher)
        def _():
            meet(place + distance)
            z_copy(0, place + distance).start()

    for b in range(1, N_BOX):

        @pl.when(b > q)
        def _():
            @pl.when(staggered)
            def _():
                pl.semaphore_wait(known_box.at[b], 1)

            x_copy(b).start()

    for p in range(OCTET):

        @pl.when((p != place) & ((p > 0) | (turned == 0) | (place == 0)))
        def _():
            z_copy(1, p).start()

    @pl.when((turned == 1) & (place > 0))
    def _():
        meet(0)
        for c in range(2):
            z_copy(c, 0).start()

    @pl.when(together)
    def _():
        for c in range(2, CHUNKS):
            for p in range(OCTET):

                @pl.when(p != place)
                def _():
                    z_copy(c, p).start()

    @pl.when(staggered & (place >= OCTET // 2))
    def _():
        for p in range(OCTET):

            @pl.when(p != place)
            def _():
                for c in range(2, CHUNKS):
                    z_copy(c, p).start()

    @pl.when(staggered & (place < OCTET // 2))
    def _():
        for c in range(2, CHUNKS):
            for p in (4, 5, 6, 7, 0, 1, 2, 3):

                @pl.when(p != place)
                def _():
                    z_copy(c, p).start()

    interp_tables(high, low)
    phase_tables(lateral, axial)

    def translation():
        for copy in (locals_[0], locals_[1], locals_[2], locals_[4]):
            copy.wait()
        for b in range(N_BOX):

            @pl.when(b != q)
            def _():
                x_arrival(b).wait_recv()


        def one_box(g, carry):
            real = jnp.zeros((SLAB, PHI), F32)
            imag = jnp.zeros((SLAB, PHI), F32)
            for k in range(FAR):
                box, kind = fb[k, g], ft[k, g]
                value = slab[box]
                factor = ops[kind].astype(F32)
                value_r, value_i = value[:, :PHI], value[:, PHI:]
                factor_r, factor_i = factor[:, :PHI], factor[:, PHI:]
                real += factor_r * value_r - factor_i * value_i
                imag += factor_r * value_i + factor_i * value_r
            incoming[0, g, :, 0:PHI] = real
            incoming[0, g, :, PHI : 2 * PHI] = imag
            return carry

        lax.fori_loop(0, GROUP, one_box, 0)

    def refine(c):
        target = upper * c + (1 - upper) * (N_BOX - 1 - c)
        if c in (0, CHUNKS - 1):
            bottom = 1 - upper if c == 0 else upper
            source = pl.multiple_of(8 + bottom * (TH - 8), 8)
            place = pl.multiple_of(bottom * (TH + 8), 8)
            for d in range(OCTET):
                rows = ext[d, pl.ds(source, 8), :]
                ext[d, pl.ds(place, 8), 0:PHI] = pltpu.roll(rows[:, :PHI], PHI // 2, 1)
                ext[d, pl.ds(place, 8), PHI : 2 * PHI] = pltpu.roll(rows[:, PHI:], PHI // 2, 1)
        window = pl.ds(pl.multiple_of(SLAB * target, 8), 2 * SLAB)
        sums = [ext[d, window, :] for d in range(OCTET)]
        for s in (1, 2, 4):
            sums = [sums[k] + sums[k ^ s] if not k & s else sums[k] - sums[k ^ s] for k in range(OCTET)]
        weights = polar_weights(target)
        rows = []
        for k in range(OCTET):
            pieces = jnp.concatenate(halves(sums[k]), axis=0)
            polar = jnp.dot(weights, pieces, preferred_element_type=F32)
            rows += [polar[:, :PHI], polar[:, PHI:]]
        stacked_high, stacked_low = halves(jnp.concatenate(rows, axis=0))
        both = jnp.concatenate([stacked_high, stacked_low], axis=1)
        wide = jnp.dot(both, high[...], preferred_element_type=F32)
        wide += jnp.dot(stacked_high, low[...], preferred_element_type=F32)
        angles = pl.ds(pl.multiple_of(2 * SLAB * target, 8), 2 * SLAB)
        parts = []
        for third in range(2):
            real, imag = 0.0, 0.0
            for k in range(4):
                at = 4 * SLAB * (4 * third + k)
                w_r = wide[at : at + 2 * SLAB]
                w_i = wide[at + 2 * SLAB : at + 4 * SLAB]
                table = lateral[k, angles, :]
                if k == 0:
                    real, imag = table * w_r, table * w_i
                elif k == 3:
                    real, imag = real - table * w_r, imag - table * w_i
                else:
                    real, imag = real - table * w_i, imag + table * w_r
            parts.append((real, imag))
        cosine, sine = axial[0, angles, :], axial[1, angles, :]
        made[c, :, 0 : 2 * PHI] = cosine * parts[0][0] - sine * parts[1][1]
        made[c, :, 2 * PHI : 4 * PHI] = cosine * parts[0][1] + sine * parts[1][0]

        @pl.when(target != q)
        def _():
            a_copy(c).start()

        @pl.when(target == q)
        def _():
            kept[q] = made[c]

    locals_[3].wait()
    for c in range(CHUNKS):
        for p in range(OCTET):

            @pl.when(p != place)
            def _():
                z_arrival(c, p).wait_recv()

        refine(c)
        if c == 1:

            @pl.when(jnp.logical_not(latest))
            def _():
                translation()

    @pl.when(latest)
    def _():
        translation()

    for e in range(1, N_BOX):
        other = box_peer(e)
        pltpu.make_async_remote_copy(
            src_ref=made.at[0],
            dst_ref=kept.at[other],
            send_sem=a_send.at[0],
            recv_sem=a_recv.at[other],
            device_id=(other, r),
            device_id_type=MESH,
        ).wait_recv()
    for c in range(CHUNKS):
        target = upper * c + (1 - upper) * (N_BOX - 1 - c)

        @pl.when(target != q)
        def _():
            a_copy(c).wait_send()

        for p in range(OCTET):

            @pl.when(p != place)
            def _():
                z_copy(c, p).wait_send()

    for b in range(N_BOX):

        @pl.when(b != q)
        def _():
            x_copy(b).wait_send()


def finish(made_inc, made_agg, incoming, aggregated, sems):
    copies = [
        pltpu.make_async_copy(made_inc, incoming, sems.at[0]),
        pltpu.make_async_copy(made_agg, aggregated, sems.at[1]),
    ]
    for copy in copies:
        copy.start()
    for copy in copies:
        copy.wait()


def shards(patterns, far_boxes, far_types, transfer):
    anywhere = pl.BlockSpec(memory_space=pltpu.HBM)
    vmem = pltpu.VMEM
    dma = pltpu.SemaphoreType.DMA
    results = pl.pallas_call(
        kernel,
        out_shape=(
            pltpu.VMEM((1, GROUP, SLAB, 2 * PHI), F32),
            pltpu.VMEM((N_BOX, 2 * SLAB, 4 * PHI), F32),
        ),
        in_specs=[anywhere] * 4,
        out_specs=(pl.BlockSpec(memory_space=vmem),) * 2,
        scratch_shapes=[
            vmem((OCTET, TH + 16, 2 * PHI), F32),
            vmem((GROUP, SLAB, 2 * PHI), F32),
            vmem(transfer.shape, BF16),
            vmem((CHUNKS, 2 * SLAB, 4 * PHI), F32),
            pltpu.SMEM((FAR, GROUP), jnp.int32),
            pltpu.SMEM((FAR, GROUP), jnp.int32),
            vmem((2 * PHI, 2 * PHI), BF16),
            vmem((PHI, 2 * PHI), BF16),
            vmem((4, 2 * TH, 2 * PHI), F32),
            vmem((2, 2 * TH, 2 * PHI), F32),
            pltpu.SemaphoreType.REGULAR((OCTET,)),
            pltpu.SemaphoreType.REGULAR((N_BOX,)),
            dma((CHUNKS, OCTET)),
            dma((CHUNKS, OCTET)),
            dma((N_BOX,)),
            dma((N_BOX,)),
            dma((CHUNKS,)),
            dma((N_BOX,)),
            dma((5,)),
        ],
        compiler_params=pltpu.CompilerParams(
            collective_id=0, has_side_effects=True, vmem_limit_bytes=56 * 1024 * 1024
        ),
    )(patterns, jnp.swapaxes(far_boxes, 1, 2), jnp.swapaxes(far_types, 1, 2), transfer)
    return pl.pallas_call(
        finish,
        out_shape=tuple(pltpu.HBM(v.shape, v.dtype) for v in results),
        in_specs=[pl.BlockSpec(memory_space=pl.ANY)] * 2,
        out_specs=(pl.BlockSpec(memory_space=pl.ANY),) * 2,
        scratch_shapes=[dma((2,))],
        compiler_params=pltpu.CompilerParams(vmem_limit_bytes=1024 * 1024),
    )(*results)


def solution(mesh):
    return jax.shard_map(
        shards,
        mesh=mesh,
        in_specs=(
            P("box", "dir", None, None),
            P("dir", None, None),
            P("dir", None, None),
            P(None, "box", None),
        ),
        out_specs=(P("dir", None, "box", None), P("dir", "box", None)),
        check_vma=False,
    )
```
